32 devices in a mesh: edges: 8 (over z, x), grp: 4 (over y, core).
Axes of the slice: x: 2, y: 2, z: 4, core: 2. Of those that a mesh axis runs over, the one named last changes fastest.
Arguments:
- features: float32 [64, 16384], P(None, ('edges', 'grp')), may hold values from -6 to 6
- positions: float32 [3, 16384], P(None, 'edges'), may hold values from -1 to 26, as said below
- lattice: float32 [3, 3], replicated, may hold values from -0.4 to 24, as said below
- neighbour_source: int32 [128, 16384], P('grp', 'edges'), may hold values from -2048 to 2048, as said below
- neighbour_image: int32 [3, 128, 16384], P(None, 'grp', 'edges'), may hold values from -1 to 1, as said below
- valid_count: int32 [16384], P('edges'), may hold values from 16 to 128, as said below
- input_proj: bfloat16 [2, 64, 64], replicated, may hold values from -0.75 to 0.75
- filter_first: bfloat16 [2, 300, 64], replicated, may hold values from -4 to 4
- filter_first_bias: float32 [2, 64], replicated, may hold values from -3 to 3
- filter_second: bfloat16 [2, 64, 64], replicated, may hold values from -0.375 to 0.375
- filter_second_bias: float32 [2, 64], replicated, may hold values from -0.6 to 0.6
- atom_first: bfloat16 [2, 64, 64], replicated, may hold values from -0.75 to 0.75
- atom_first_bias: float32 [2, 64], replicated, may hold values from -2 to 2
- atom_second: bfloat16 [2, 64, 64], replicated, may hold values from -0.75 to 0.75
- atom_second_bias: float32 [2, 64], replicated, may hold values from -2 to 2
- cotangent: float32 [64, 16384], P(None, ('edges', 'grp')), may hold values from -6 to 6
Outputs:
- new_features: float32 [64, 16384], P(None, ('edges', 'grp'))
- feature_grad: float32 [64, 16384], P(None, ('edges', 'grp'))
- input_proj_grad: float32 [2, 64, 64], replicated
- filter_first_grad: float32 [2, 300, 64], replicated
- filter_first_bias_grad: float32 [2, 64], replicated
- filter_second_grad: float32 [2, 64, 64], replicated
- filter_second_bias_grad: float32 [2, 64], replicated
- atom_first_grad: float32 [2, 64, 64], replicated
- atom_first_bias_grad: float32 [2, 64], replicated
- atom_second_grad: float32 [2, 64, 64], replicated
- atom_second_bias_grad: float32 [2, 64], replicated
The draws below stay inside these ranges and needn't reach their ends.
Inputs may be any that keep to these rules, and one draw needn't show every extreme that they name: `neighbour_source`: entry [j, t] is a nonzero k: the source is atom (t + k) modulo 16384, in the slab of 2048 atoms that holds t or in one of the two slabs beside it, cyclically. `neighbour_image`: component 0 is -1 where t + neighbour_source[j, t] < 0, 1 where it is >= 16384 and 0 otherwise; components 1 and 2 take any of the three values. `valid_count`: slots below the count hold neighbours; the others are padding. Some atom of every slab has 128. `positions`: atom t lies at fractional coordinates ((t + u) / 16384, v, w) of the cell, u, v, w in [0, 1). `lattice`: lower triangular; the diagonal is 24, 1.5, 1.5.
All inputs are finite; a program needn't handle non-finite values.
Results may differ from the reference program's by a relative error of at most 0.019.
Values may be sent and summed in bfloat16 or wider, within the bound.
No kernel may reach another device: no remote copies, remote signals or barrier semaphores. Data moves between devices by JAX's collectives and lax.ppermute only.
A program may use at most 128 MiB of HBM per device.

```python
import math
import jax
import jax.numpy as jnp
from jax import lax

FEAT = 64
NRBF = 300
SLOTS = 128
LAYERS = 2
SLAB = 2048
ATOMS = 16384


def draw_offsets(key):
    base = jax.random.fold_in(key, 101)
    magnitude = jax.random.randint(base, (SLOTS, ATOMS), 1, SLAB + 1)
    sign_bits = jax.random.randint(jax.random.fold_in(base, 1), (SLOTS, ATOMS), 0, 2)
    return magnitude * (2 * sign_bits - 1)


def lattice_matrix(key):
    base = jax.random.fold_in(key, 202)
    shear = jax.random.uniform(base, (3,), jnp.float32, -0.4, 0.4)
    length = 3.0 * (ATOMS // SLAB)
    matrix = jnp.zeros((3, 3), jnp.float32)
    matrix = matrix.at[0, 0].set(length).at[1, 1].set(1.5).at[2, 2].set(1.5)
    matrix = matrix.at[1, 0].set(shear[0]).at[2, 0].set(shear[1]).at[2, 1].set(shear[2])
    return matrix


def draw_neighbour_source(key, part):
    offsets = draw_offsets(key)
    return offsets.astype(jnp.int32)


def draw_neighbour_image(key, part):
    offsets = draw_offsets(key)
    key = jax.random.fold_in(key, 5)
    reach = jnp.arange(ATOMS, dtype=jnp.int32)[None, :] + offsets
    first_axis = jnp.where(reach < 0, -1, jnp.where(reach >= ATOMS, 1, 0))
    others = jax.random.randint(key, (2, SLOTS, ATOMS), -1, 2)
    return jnp.concatenate([first_axis[None], others], axis=0).astype(jnp.int32)


def draw_valid_count(key, part):
    key = jax.random.fold_in(key, 7)
    counts = jax.random.randint(key, (ATOMS,), SLOTS // 8, SLOTS + 1)
    return counts.at[::SLAB].set(SLOTS).astype(jnp.int32)


def draw_positions(key, part):
    matrix = lattice_matrix(key)
    key = jax.random.fold_in(key, 9)
    along = (jnp.arange(ATOMS).astype(jnp.float32) + jax.random.uniform(key, (ATOMS,), jnp.float32)) / ATOMS
    rest = jax.random.uniform(jax.random.fold_in(key, 1), (2, ATOMS), jnp.float32)
    columns = []
    for axis_id in range(3):
        columns.append(along * matrix[0, axis_id] + rest[0] * matrix[1, axis_id] + rest[1] * matrix[2, axis_id])
    return jnp.stack(columns, axis=0).astype(jnp.float32)


def draw_lattice(key, part):
    matrix = lattice_matrix(key)
    return matrix


def shard_levels(own_key, extent, split, smallest, top_value):
    def one(position, shards_of):
        steps = jax.random.uniform(jax.random.fold_in(jax.random.fold_in(own_key, 6), position), (shards_of,), jnp.float32, smallest / len(split), top_value / len(split))
        return jnp.repeat(jnp.exp(steps), extent[position] // shards_of).reshape((-1,) + (1,) * (len(extent) - position - 1))

    factor_of = one(*split[0])
    for cut in split[1:]:
        factor_of = factor_of * one(*cut)
    return factor_of


def noise(own_key, dims, deviation, most, shards=(), held_as=jnp.bfloat16):
    values = jax.random.normal(own_key, dims, jnp.float32) * deviation
    if len(shards) > 0:
        values = shard_levels(own_key, dims, shards, -0.22, 0.18) * values
    return jnp.clip(values, min=-most, max=most).astype(held_as)


def setup_inputs(seed: int = 0) -> dict:
    seeds = jax.random.split(jax.random.key(seed), 17)
    return {
        "features": noise(seeds[0], (FEAT, ATOMS), 1.0, 6.0, ((1, 32),), jnp.float32),
        "positions": draw_positions(jax.random.fold_in(seeds[16], 71), 0),
        "lattice": draw_lattice(jax.random.fold_in(seeds[16], 71), 0),
        "neighbour_source": draw_neighbour_source(jax.random.fold_in(seeds[16], 71), 0),
        "neighbour_image": draw_neighbour_image(jax.random.fold_in(seeds[16], 71), 0),
        "valid_count": draw_valid_count(jax.random.fold_in(seeds[16], 71), 0),
        "input_proj": noise(seeds[6], (LAYERS, FEAT, FEAT), FEAT ** -0.5, 0.75),
        "filter_first": noise(seeds[7], (LAYERS, NRBF, FEAT), 2 ** -0.5, 4.0),
        "filter_first_bias": noise(seeds[8], (LAYERS, FEAT), 0.5, 3.0, (), jnp.float32),
        "filter_second": noise(seeds[9], (LAYERS, FEAT, FEAT), (4 * FEAT) ** -0.5, 0.375),
        "filter_second_bias": noise(seeds[10], (LAYERS, FEAT), 0.1, 0.6, (), jnp.float32),
        "atom_first": noise(seeds[11], (LAYERS, FEAT, FEAT), FEAT ** -0.5, 0.75),
        "atom_first_bias": noise(seeds[12], (LAYERS, FEAT), 0.3, 2.0, (), jnp.float32),
        "atom_second": noise(seeds[13], (LAYERS, FEAT, FEAT), FEAT ** -0.5, 0.75),
        "atom_second_bias": noise(seeds[14], (LAYERS, FEAT), 0.3, 2.0, (), jnp.float32),
        "cotangent": noise(seeds[15], (FEAT, ATOMS), 1.0, 6.0, ((1, 32),), jnp.float32),
    }


RADIUS = 5.0
LOG_TWO = math.log(2.0)
HIGHEST = lax.Precision.HIGHEST

@jax.custom_vjp
def low(v):
    return lax.optimization_barrier(v.astype(jnp.bfloat16)).astype(jnp.float32)

@jax.custom_vjp
def low_back(v):
    return v

def low_keep(v):
    return (low(v), None)

def low_pass(kept, grad):
    return (grad,)

def back_keep(v):
    return (v, None)

def back_low(kept, grad):
    return (low(grad),)
low.defvjp(low_keep, low_pass)
low_back.defvjp(back_keep, back_low)

def shifted(argument):
    return jax.nn.softplus(argument) - LOG_TWO

def expand(distance, nbasis):
    spacing = RADIUS / (nbasis - 1)
    centers = jnp.arange(nbasis).astype(distance.dtype) * spacing
    scaled = (distance[None, :] - centers[:, None]) / spacing
    return jnp.exp(-0.5 * scaled * scaled)

def edge_weights(source_pos, target_pos, image_rows, lattice, slot_ids, count_rows):
    image_float = image_rows.astype(source_pos.dtype)
    components = []
    for axis_id in range(3):
        shift_part = image_float[0] * lattice[0, axis_id] + image_float[1] * lattice[1, axis_id] + image_float[2] * lattice[2, axis_id]
        components.append(source_pos[axis_id] + shift_part - target_pos[axis_id])
    distance = jnp.sqrt(components[0] * components[0] + components[1] * components[1] + components[2] * components[2])
    cutoff = jnp.where(distance < RADIUS, 0.5 * (jnp.cos(math.pi * distance / RADIUS) + 1.0), 0.0)
    slot_live = (slot_ids[:, None] < count_rows[None, :]).reshape(-1).astype(source_pos.dtype)
    return (distance, cutoff * slot_live)

def reference(features, positions, lattice, neighbour_source, neighbour_image, valid_count, input_proj, filter_first, filter_first_bias, filter_second, filter_second_bias, atom_first, atom_first_bias, atom_second, atom_second_bias, cotangent):
    slot_total, atom_total = neighbour_source.shape
    feat_width = features.shape[0]
    nbasis = filter_first.shape[1]
    block_width = math.gcd(atom_total, 64)
    block_count = atom_total // block_width
    source_blocks = neighbour_source.reshape(slot_total, block_count, block_width).transpose(1, 0, 2)
    image_blocks = neighbour_image.reshape(3, slot_total, block_count, block_width).transpose(2, 0, 1, 3)
    count_blocks = valid_count.reshape(block_count, block_width)
    target_blocks = positions.reshape(3, block_count, block_width).transpose(1, 0, 2)
    id_blocks = jnp.arange(atom_total, dtype=jnp.int32).reshape(block_count, block_width)
    slot_ids = jnp.arange(slot_total, dtype=jnp.int32)

    def forward(state_rows, proj_weight, first_weight, first_bias, second_weight, second_bias, atom_one, atom_one_bias, atom_two, atom_two_bias):
        for layer_id in range(proj_weight.shape[0]):
            source_rows = low(low_back(jnp.einsum('fc,fa->ca', proj_weight[layer_id], low(state_rows), precision=HIGHEST)))

            def edge_block(inputs, layer_id=layer_id, source_rows=source_rows):
                offset_index, image_index, count_index, target_pos, target_ids = inputs
                flat_index = jnp.remainder(offset_index + target_ids[None, :], atom_total).astype(jnp.int32).reshape(-1)
                distance, edge_weight = edge_weights(jnp.take(positions, flat_index, axis=1), jnp.tile(target_pos, (1, slot_total)), image_index.reshape(3, -1), lattice, slot_ids, count_index)
                basis_rows = low(expand(distance, nbasis))
                hidden_pre = low_back(jnp.einsum('kc,ke->ce', first_weight[layer_id], basis_rows, precision=HIGHEST) + first_bias[layer_id][:, None])
                hidden = low(shifted(hidden_pre))
                filter_pre = low_back(jnp.einsum('co,ce->oe', second_weight[layer_id], hidden, precision=HIGHEST) + second_bias[layer_id][:, None])
                message = jnp.take(source_rows, flat_index, axis=1) * (filter_pre * edge_weight)
                return message.reshape(feat_width, slot_total, -1).sum(axis=1)
            blocks_out = lax.map(jax.checkpoint(edge_block), (source_blocks, image_blocks, count_blocks, target_blocks, id_blocks))
            pooled = low(low_back(blocks_out.transpose(1, 0, 2).reshape(feat_width, atom_total)))
            atom_pre = low_back(jnp.einsum('io,ia->oa', atom_one[layer_id], pooled, precision=HIGHEST) + atom_one_bias[layer_id][:, None])
            atom_hidden = low(shifted(atom_pre))
            branch = low_back(jnp.einsum('io,ia->oa', atom_two[layer_id], atom_hidden, precision=HIGHEST) + atom_two_bias[layer_id][:, None])
            state_rows = state_rows + branch
        return state_rows
    result, pullback = jax.vjp(forward, features, input_proj.astype(jnp.float32), filter_first.astype(jnp.float32), filter_first_bias, filter_second.astype(jnp.float32), filter_second_bias, atom_first.astype(jnp.float32), atom_first_bias, atom_second.astype(jnp.float32), atom_second_bias)
    gradients = pullback(cotangent)
    return (result, gradients[0], gradients[1], gradients[2], gradients[3], gradients[4], gradients[5], gradients[6], gradients[7], gradients[8], gradients[9])
```

```python
import functools
import math

import jax
import jax.numpy as jnp
from jax import lax
from jax.experimental import pallas as pl
from jax.experimental.pallas import tpu as pltpu
from jax.sharding import PartitionSpec as P

RADIUS = 5.0
LN2 = math.log(2.0)
LOG2E = 1.0 / LN2
LANES = 128
DEAD = (1 << 31) - 1
LIVE_BOUND = 1 << 30
F32 = jnp.float32
BF16 = jnp.bfloat16
MIB = 1 << 20

FIRST, LAST, HALF, COUNT = 0, 1, 2, 3
PASS = 8
QUAD = 4


def dot(lhs, rhs):
    return jnp.dot(lhs, rhs, preferred_element_type=F32)


def dot_nt(lhs, rhs):
    return lax.dot_general(lhs, rhs, (((1,), (1,)), ((), ())), preferred_element_type=F32)


def turned(weight):
    return weight.astype(F32).T.astype(weight.dtype)


def column(row, rows, cols=LANES):
    return jnp.broadcast_to(row, (cols, rows)).T


def widened(col_block, times):
    return jnp.concatenate([col_block] * times, axis=1)


def partner(x, axis, step):
    rest = tuple(a for a in range(3) if a != axis)
    numbers = lax.GatherDimensionNumbers(
        offset_dims=(),
        collapsed_slice_dims=(axis,),
        start_index_map=(axis,),
        operand_batching_dims=rest,
        start_indices_batching_dims=rest,
    )
    index = lax.broadcasted_iota(jnp.int32, x.shape, axis) ^ step
    mode = lax.GatherScatterMode.PROMISE_IN_BOUNDS
    return lax.gather(x, index[..., None], numbers, slice_sizes=(1, 1, 1), mode=mode)


def bitonic(x, vbits):
    count = 1 << vbits
    total = vbits + 10
    si = lax.broadcasted_iota(jnp.int32, (1, 8, LANES), 1)
    li = lax.broadcasted_iota(jnp.int32, (1, 8, LANES), 2)

    def bit(k):
        if k < vbits + 3:
            return (si >> (k - vbits)) & 1
        return (li >> (k - vbits - 3)) & 1

    def flip(x, k):
        if k >= total:
            return x
        if k < vbits:
            a = x.reshape(count >> (k + 1), 2, 1 << k, 8, LANES)
            return jnp.stack([a[:, 0], ~a[:, 1]], axis=1).reshape(count, 8, LANES)
        return x ^ (-bit(k))

    for k in range(1, total + 1):
        x = flip(x, k)
        for j in range(k - 1, vbits + 2 if k == total else -1, -1):
            if j < vbits:
                a = x.reshape(count >> (j + 1), 2, 1 << j, 8, LANES)
                low = jnp.minimum(a[:, 0], a[:, 1])
                high = jnp.maximum(a[:, 0], a[:, 1])
                x = jnp.stack([low, high], axis=1).reshape(count, 8, LANES)
            else:
                if j < vbits + 3:
                    step, axis = 1 << (j - vbits), 1
                else:
                    step, axis = 1 << (j - vbits - 3), 2
                other = partner(x, axis, step)
                upper = jnp.broadcast_to(bit(j) == 1, x.shape)
                x = jnp.where(upper, jnp.maximum(x, other), jnp.minimum(x, other))
        x = flip(x, k)
    return x


def make_key(source, target, images, source_bits, own_bits):
    low_bits = own_bits - 1
    half = target >> low_bits
    field = source ^ (-half & ((1 << source_bits) - 1))
    low = target & ((1 << low_bits) - 1)
    return (((((half << source_bits) | field) << low_bits) | low) << 4) | images


def split_key(key, source_bits, own_bits):
    low_bits = own_bits - 1
    half = key >> (source_bits + low_bits + 4)
    field = (key >> (low_bits + 4)) & ((1 << source_bits) - 1)
    source = field ^ (-half & ((1 << source_bits) - 1))
    return source, ((key >> 4) & ((1 << low_bits) - 1)) | (half << low_bits)


def sort_kernel(reach, source_bits, own_bits, rank_ref, words_ref, valid_ref, keys_ref, stats_ref, keys, sem):
    def whole(which):
        parts = [words_ref[g, which].astype(jnp.int32) for g in range(words_ref.shape[0])]
        return jnp.concatenate(parts, axis=0)

    offset = whole(0)
    own = offset.shape[1]
    target = lax.broadcasted_iota(jnp.int32, offset.shape, 1)
    slot = lax.broadcasted_iota(jnp.int32, offset.shape, 0)
    source = target + offset + reach
    images = ((whole(1) + 1) << 2) | (whole(2) + 1)
    key = make_key(source, target, images, source_bits, own_bits)
    valid = valid_ref[:, pl.ds(pl.multiple_of(rank_ref[0] * own, LANES), own)]
    key = jnp.where(slot < valid, key, DEAD)
    tiles = [key[:, i * LANES : (i + 1) * LANES].reshape(-1, 8, LANES) for i in range(own // LANES)]
    cube = jnp.concatenate(tiles, axis=0)
    count = cube.shape[0]
    cube = bitonic(cube, count.bit_length() - 1)

    bound = 1 << (source_bits + own_bits + 3)
    rows = cube.reshape(count * 8, LANES).T
    low_rows = jnp.where(rows < bound, rows, DEAD)
    high_rows = jnp.where(rows < bound, DEAD, rows)
    has_low = jnp.min(rows, axis=1, keepdims=True) < bound
    shifted = pltpu.roll(high_rows, 1, 0)
    keys[0:LANES, :] = jnp.where(has_low, low_rows, shifted)
    tail = jnp.where(lax.broadcasted_iota(jnp.int32, (8, rows.shape[1]), 0) == 0, shifted[0:8], DEAD)
    keys[LANES : LANES + 8, :] = tail
    copy = pltpu.make_async_copy(keys, keys_ref, sem)
    copy.start()

    source, target = split_key(cube, source_bits, own_bits)
    block = source >> 7
    in_low = cube < bound
    in_high = jnp.logical_not(in_low) & (cube < LIVE_BOUND)

    def over(reduce, value):
        return reduce(reduce(value, axis=0), axis=0, keepdims=True)

    def stats_of(inside):
        some = over(jnp.max, jnp.where(inside, 1, 0))
        first = over(jnp.min, jnp.where(inside, block, DEAD))
        last = over(jnp.max, jnp.where(inside, block, 0))
        return some, jnp.where(some == 1, first, 0), last

    some, first, last = stats_of(in_low)
    moved_on = [pltpu.roll(jnp.broadcast_to(x, (8, LANES)), 1, 1)[0:1] for x in stats_of(in_high)]
    lane = lax.broadcasted_iota(jnp.int32, (1, LANES), 1)
    low = some == 1
    whole = [jnp.where(low, x, y) for x, y in zip((some, first, last), moved_on)]
    extra = [jnp.where(lane == 0, x, 0) for x in moved_on]
    numbers = jnp.maximum(whole[0] * (lane + 1), extra[0] * (LANES + 1))
    chunks = jnp.max(numbers.astype(F32), axis=1, keepdims=True).astype(jnp.int32)
    stats_ref[...] = jnp.zeros(stats_ref.shape, jnp.int32)
    for line, near, far in ((FIRST, whole[1], extra[1]), (LAST, whole[2], extra[2])):
        stats_ref[line : line + 1, 0:LANES] = near
        stats_ref[line : line + 1, LANES : 2 * LANES] = far
    stats_ref[HALF : HALF + 1, 0:LANES] = jnp.where(low, 0, 1)
    stats_ref[HALF : HALF + 1, LANES : 2 * LANES] = jnp.ones((1, LANES), jnp.int32)
    stats_ref[COUNT : COUNT + 1, 0:LANES] = jnp.broadcast_to(chunks, (1, LANES))
    copy.wait()


def send_kernel(rank_ref, offset_ref, image_ref, features_ref, positions_ref, words_ref, block_ref):
    group, _, _, own = words_ref.shape
    feat = features_ref.shape[0]
    for g in range(group):
        span = slice(g * own, (g + 1) * own)
        words_ref[g, 0] = offset_ref[:, span].astype(jnp.int16)
        words_ref[g, 1] = image_ref[1, :, span].astype(jnp.int16)
        words_ref[g, 2] = image_ref[2, :, span].astype(jnp.int16)
    mine = positions_ref[:, pl.ds(pl.multiple_of(rank_ref[0] * own, LANES), own)]
    high = mine.astype(BF16).astype(F32)
    middle = (mine - high).astype(BF16).astype(F32)
    low = mine - high - middle
    rest = block_ref.shape[0] - feat - 9
    tail = [high, middle, low, jnp.zeros((rest, own), F32)]
    block_ref[0:feat, :] = features_ref[...].astype(BF16)
    block_ref[feat:, :] = jnp.concatenate(tail, axis=0).astype(BF16)


class Flow:
    def __init__(self, far, near, sem, store=False, kept=False):
        self.far, self.near, self.sem = far, near, sem
        self.store, self.kept = store, kept

    def copy(self, p, slot):
        far = self.far.at[pl.ds(p * PASS, PASS)]
        near = self.near.at[pl.ds(p * PASS, PASS)] if self.kept else self.near.at[slot]
        source, target = (near, far) if self.store else (far, near)
        return pltpu.make_async_copy(source, target, self.sem.at[slot])


def start_first(loads):
    for flow in loads:
        flow.copy(0, 0).start()


def flow_loop(count, loads, stores, body):
    def step(p, carry):
        slot = lax.rem(p, 2)

        @pl.when(p + 1 < count)
        def _():
            for flow in loads:
                flow.copy(p + 1, 1 - slot).start()

        for flow in loads:
            flow.copy(p, slot).wait()

        @pl.when(p >= 2)
        def _():
            for flow in stores:
                flow.copy(p - 2, slot).wait()

        body(p, slot)
        for flow in stores:
            flow.copy(p, slot).start()
        return carry

    lax.fori_loop(0, count, step, 0)


def wait_last(count, stores):
    @pl.when(count >= 2)
    def _():
        for flow in stores:
            flow.copy(count - 2, lax.rem(count, 2)).wait()

    for flow in stores:
        flow.copy(count - 1, lax.rem(count + 1, 2)).wait()


def pass_count(info_ref):
    return (info_ref[COUNT, 0] + PASS - 1) // PASS


class Mode:
    def __init__(self, static, loop):
        self.static, self.loop = static, loop


def reach_of(items):
    return functools.reduce(jnp.maximum, [last - first for _, _, first, last, _ in items])


def interleave(tracks):
    waiting, running = list(tracks), []
    while waiting or running:
        if waiting:
            running.append(waiting.pop(0))
        for track in list(running):
            if next(track, track) is track:
                running.remove(track)


def items_of(p, info_ref):
    items = []
    for u in range(PASS):
        i = p * PASS + u
        items.append((u, i, info_ref[FIRST, i], info_ref[LAST, i], info_ref[HALF, i]))
    return items


def is_whole(p, info_ref):
    live = info_ref[COUNT, 0] - p * PASS
    return (reach_of(items_of(p, info_ref)) <= 1) & (live > QUAD)


def mixed(tracks, others):
    out = []
    for i in range(max(len(tracks), len(others))):
        out += others[i : i + 1] + tracks[i : i + 1]
    return out


def each_pass(p, info_ref, chunk, pooling=None, beside=None):
    items = items_of(p, info_ref)
    live = info_ref[COUNT, 0] - p * PASS
    whole = is_whole(p, info_ref)
    before = jnp.maximum(p - 1, 0)
    simple_mode = Mode(2, False)

    def earlier():
        return [] if pooling is None else pooling.settle_list(items_of(before, info_ref), before)

    @pl.when(whole)
    def _():
        tracks = mixed([chunk(item, simple_mode) for item in items], earlier())
        if beside is not None:
            tracks.insert(2, beside())
        interleave(tracks)

    @pl.when(jnp.logical_not(whole))
    def _():
        for start in range(0, PASS, QUAD):
            quad = items[start : start + QUAD]
            reach = reach_of(quad)
            some = live > start

            @pl.when(some & (reach <= 1))
            def _(quad=quad, start=start):
                work = [chunk(item, simple_mode) for item in quad]
                interleave(mixed(work, earlier() if start == 0 else []))

            @pl.when(some & (reach > 1))
            def _(quad=quad, start=start, reach=reach):
                if start == 0:
                    interleave(earlier())

                @pl.when(reach <= 3)
                def _():
                    interleave([chunk(item, Mode(4, False)) for item in quad])

                @pl.when(reach > 3)
                def _():
                    for item in quad:
                        interleave([chunk(item, Mode(2, True))])

            if pooling is not None:

                @pl.when(some)
                def _(quad=quad):
                    interleave(pooling.settle_list(quad, p))

        if pooling is not None:

            @pl.when(live > PASS)
            def _():
                pooling.clear()


def one_hots(row, blocks, ids):
    low = row & (LANES - 1)
    high = row >> 7
    ids = widened(ids, row.shape[1] // LANES)
    parts = []
    for b in blocks:
        within = low if b is None else jnp.where(high == b, low, -1)
        within = jnp.broadcast_to(within.astype(F32).astype(BF16), ids.shape)
        parts.append(jnp.where(ids == within, BF16(1), BF16(0)))
    return jnp.concatenate(parts, axis=0)


def row_numbers():
    return lax.broadcasted_iota(jnp.int32, (LANES, LANES), 0).astype(F32).astype(BF16)


def split_rows(value, row, blocks):
    high = row >> 7
    return jnp.concatenate(
        [value * jnp.where(high == b, 1.0, 0.0).astype(BF16) for b in blocks], axis=0
    )


def gather_lanes(table, index):
    numbers = lax.GatherDimensionNumbers(
        offset_dims=(),
        collapsed_slice_dims=(1,),
        start_index_map=(1,),
        operand_batching_dims=(0,),
        start_indices_batching_dims=(0,),
    )
    mode = lax.GatherScatterMode.PROMISE_IN_BOUNDS
    return lax.gather(table, index[..., None], numbers, slice_sizes=(1, 1), mode=mode)


def gather_block(table, row, fill=None, block=None):
    low = (row & (LANES - 1)).astype(jnp.int16)
    flag = None if fill is None else jnp.where((row >> 7) == block, 1.0, 0.0).astype(BF16)
    parts = []
    for q in range(row.shape[1] // LANES):
        span = slice(q * LANES, (q + 1) * LANES)
        got = gather_lanes(table, jnp.broadcast_to(low[:, span], table.shape))
        if fill is not None:
            inside = jnp.broadcast_to(flag[:, span], got.shape) > BF16(0.5)
            got = jnp.where(inside, got, fill[:, span])
        parts.append(got)
    return joined(parts)


def gather_sources(table_ref, row, first, last, mode):
    got = gather_block(table_ref[first], row)
    for b in range(1, mode.static):
        got = gather_block(table_ref[first + b], row, got, first + b)
    if not mode.loop:
        return got
    return lax.fori_loop(
        first + mode.static,
        last + 1,
        lambda b, acc: gather_block(table_ref[b], row, acc, b),
        got,
    )


def gather_targets(table_ref, row, half):
    blocks = table_ref.shape[0] // 2
    got = gather_block(table_ref[half * blocks], row)
    for b in range(1, blocks):
        place = half * blocks + b
        got = gather_block(table_ref[place], row, got, place)
    return got


def store_targets(table_ref, value):
    for b in range(table_ref.shape[0]):
        table_ref[b] = value[:, b * LANES : (b + 1) * LANES]


def add_to_targets(total_ref, message, row, half, ids):
    blocks = total_ref.shape[2] // message.shape[0]
    parts = split_rows(message, row, [half * blocks + b for b in range(blocks)])
    total_ref[half] += dot_nt(one_hots(row, (None,), ids), parts)


class Pooling:
    def __init__(self, total, message, target_of, info_ref, ids):
        self.total, self.message, self.target_of = total, message, target_of
        self.info_ref, self.ids = info_ref, ids
        total[...] = jnp.zeros(total.shape, F32)
        self.clear()

    def span(self, u):
        width = self.message.shape[1] // PASS
        return slice(u * width, (u + 1) * width)

    def clear(self):
        self.message[...] = jnp.zeros(self.message.shape, BF16)

    def settle(self, p, u, half):
        message = self.message[:, self.span(u)]
        row = self.target_of(p * PASS + u)
        yield
        add_to_targets(self.total, message, row, half, self.ids[...])
        yield

    def settle_list(self, items, p):
        return [self.settle(p, u, half) for u, _, _, _, half in items]

    def finish(self, p):
        @pl.when(is_whole(p, self.info_ref))
        def _():
            interleave(self.settle_list(items_of(p, self.info_ref), p))

    def rows(self):
        feat = self.message.shape[0]
        parts = []
        for half in range(self.total.shape[0]):
            turned_total = self.total[half].T
            for b in range(turned_total.shape[0] // feat):
                parts.append(turned_total[b * feat : (b + 1) * feat])
        return joined(parts).astype(BF16)


def add_to_sources(total_ref, value, row, first, last, mode, ids):
    rows = value.shape[0]
    ones = one_hots(row, (None,), ids)
    places = [first + b for b in range(mode.static)]
    sums = dot_nt(split_rows(value, row, places), ones)
    for b, place in enumerate(places):
        total_ref[place] += sums[b * rows : (b + 1) * rows]
    if not mode.loop:
        return

    def more(b, carry):
        total_ref[b] += dot_nt(split_rows(value, row, (b,)), ones)
        return carry

    lax.fori_loop(first + mode.static, last + 1, more, 0)


def build_sources(table_ref, proj, state_refs):
    flipped = turned(proj)
    tiles = state_refs[0].shape[1] // LANES
    for j, state_ref in enumerate(state_refs):
        rows = dot(flipped, state_ref[0 : proj.shape[0], :]).astype(BF16)
        for q in range(tiles):
            table_ref[j * tiles + q] = rows[:, q * LANES : (q + 1) * LANES]
    for last in range(len(state_refs) * tiles, table_ref.shape[0]):
        table_ref[last] = jnp.zeros(table_ref.shape[1:], BF16)


def source_product(state_refs, total_ref, out_refs):
    tiles = state_refs[0].shape[1] // LANES
    feat = total_ref.shape[1]
    acc = 0.0
    for j, (state_ref, out_ref) in enumerate(zip(state_refs, out_refs)):
        sums = joined([total_ref[j * tiles + q] for q in range(tiles)]).astype(BF16)
        out_ref[...] = sums
        acc = acc + dot_nt(state_ref[0:feat, :], sums)
    return acc


def ssp(value):
    return jnp.maximum(value, 0.0) + jnp.log(1.0 + jnp.exp(-jnp.abs(value))) - LN2


def sigmoid(value):
    return 1.0 / (1.0 + jnp.exp(-value))


def atom_forward(pooled, first, first_bias, second, second_bias):
    feat, own = pooled.shape
    tiles = own // LANES
    pre = dot(turned(first), pooled) + widened(column(first_bias, feat), tiles)
    hidden = ssp(pre).astype(BF16)
    branch = dot(turned(second), hidden) + widened(column(second_bias, feat), tiles)
    return pre, hidden, branch


def atom_backward(grad, pooled, pre, hidden, first, second, pack_ref):
    feat, own = grad.shape
    ones = jnp.ones((8, own), BF16)
    part = feat + 8
    out_grad = grad.astype(BF16)
    pre_grad = (dot(second, out_grad) * sigmoid(pre)).astype(BF16)
    pack_ref[part : part + feat, :] = dot_nt(pooled, pre_grad)
    pack_ref[part + feat : 2 * part, :] = dot_nt(ones, pre_grad)
    pack_ref[2 * part : 2 * part + feat, :] = dot_nt(hidden, out_grad)
    pack_ref[2 * part + feat : 3 * part, :] = dot_nt(ones, out_grad)
    return dot(first, pre_grad).astype(BF16)


LIFT = 72.0


def spans(padded):
    count = padded // 8
    parts = -(-count // 10)
    edges = [i * count // parts for i in range(parts + 1)]
    return list(zip(edges[:-1], edges[1:]))


def radial(dist_row, starts, nbasis, padded, ones_below):
    count = padded // 8
    width = dist_row.shape[1]
    where = dist_row * ((nbasis - 1) / RADIUS) - widened(starts, width // LANES)
    rows = [None] * count
    for low, high in spans(padded):
        mid = (low + high) // 2
        y = jnp.clip(where - float(mid), -60.0, 60.0)
        peak = jnp.exp2(LIFT * LOG2E - y * y * (0.5 * LOG2E))
        up = jnp.exp2(y * LOG2E)
        down = jnp.exp2(y * -LOG2E)
        for direction, ratio in ((range(mid, high), up), (range(mid - 1, low - 1, -1), down)):
            value = peak
            for v in direction:
                if v != mid:
                    value = value * ratio
                rows[v] = value * math.exp(-0.5 * (v - mid) ** 2 - LIFT)
    if ones_below:
        sublane = lax.broadcasted_iota(jnp.int32, rows[0].shape, 0)
        for v in range(count):
            if 7 * count + v >= nbasis:
                rows[v] = jnp.where(sublane == 7, 1.0, rows[v])
    return jnp.concatenate(rows, axis=0).astype(BF16)


def row_starts(padded):
    sublane = lax.broadcasted_iota(jnp.int32, (8, LANES), 0)
    return (sublane * (padded // 8)).astype(F32)


def row_order(padded):
    centre = lax.broadcasted_iota(jnp.int32, (padded, padded), 0)
    row = lax.broadcasted_iota(jnp.int32, (padded, padded), 1)
    return jnp.where(centre == (row & 7) * (padded // 8) + (row >> 3), 1.0, 0.0)


LN2_HIGH = 177 / 256
LN2_LOW = LN2 - LN2_HIGH


def activation(scaled):
    grown = jnp.exp2(scaled)
    more = grown + BF16(1)
    level = jnp.log2(more) - BF16(1)
    hidden = level * BF16(LN2_HIGH) + level * BF16(LN2_LOW)
    return hidden, grown * pltpu.reciprocal(more, approx=True)


def joined(values):
    return jnp.concatenate(values, axis=1)


def second_grads(hidden, slope, grad, weight, second_total):
    low = dot(weight, grad).astype(BF16) * slope
    tall = jnp.concatenate([hidden, jnp.ones((16, grad.shape[1]), BF16)], axis=0)
    second_total[...] += dot_nt(tall, grad)
    return low


def write_packs(out_ref, flat, first_total, packs):
    padded, both = first_total.shape
    feat = both // len(packs)
    ordered = dot(row_order(padded).astype(BF16), first_total[...].astype(BF16))
    flat[...] = jnp.zeros(flat.shape, F32)
    for l, pack in enumerate(packs):
        base = l * padded
        flat[base : base + padded, 0:feat] = ordered[:, l * feat : (l + 1) * feat]
        flat[base : base + pack.shape[0], feat : 2 * feat] = pack
    devices, share, _ = out_ref.shape

    for d in range(devices):
        out_ref[d] = flat[d * share : (d + 1) * share, :].astype(BF16)


def sums_views(ends_refs, pair_refs, feat):
    group = len(pair_refs) + 1
    views = [None] * (2 * group + 1)
    views[0], views[group], views[2 * group] = ends_refs
    for s, pair_ref in enumerate(pair_refs, 1):
        views[s] = pair_ref.at[0:feat]
        views[group + s] = pair_ref.at[feat : 2 * feat]
    return views


def gathered_sums(rank_ref, lower_ref, own_ref, upper_ref, pair_refs, sum_ref, below_ref, above_ref):
    feat = own_ref.shape[0]
    low = lower_ref[...].astype(F32)
    mine = own_ref[...].astype(F32)
    high = upper_ref[...].astype(F32)
    for s, pair_ref in enumerate(pair_refs, 1):
        straight = jnp.where(rank_ref[0] >= s, 1.0, 0.0)
        head = pair_ref[0:feat, :].astype(F32)
        tail = pair_ref[feat : 2 * feat, :].astype(F32)
        mine = mine + straight * tail + (1.0 - straight) * head
        low = low + straight * head
        high = high + (1.0 - straight) * tail
    sum_ref[...] = mine
    below_ref[...] = low.astype(BF16)
    above_ref[...] = high.astype(BF16)


def first_kernel(
    source_bits,
    own_bits,
    nbasis,
    devices,
    state_refs,
    info_ref,
    lattice_ref,
    device_ref,
    keys_ref,
    own_ref,
    proj_ref,
    ff_ref,
    ffb_ref,
    fs_ref,
    fsb_ref,
    af_ref,
    afb_ref,
    as_ref,
    asb_ref,
    dist_ref,
    weight_ref,
    hidden_far,
    slope_far,
    filter_far,
    rows_far,
    pre_far,
    next_ref,
    low_ref,
    kept_ref,
    ids,
    window_ref,
    table,
    total,
    message,
    starts,
    first_w,
    second_w,
    second_b,
    hidden_buf,
    slope_buf,
    filter_buf,
    rows_buf,
    pre_buf,
    sems,
):
    layers, feat, _ = ff_ref.shape
    own = own_ref.shape[1]
    tiles = own // LANES
    tiles_wide = keys_ref.shape[1] // LANES

    ids[...] = row_numbers()
    build_sources(table, proj_ref[0], state_refs)
    window_ref[...] = jnp.zeros(window_ref.shape, F32)
    center = len(state_refs) // 2
    for j, state_ref in enumerate(state_refs):
        place = device_ref[0] + j - center
        turn = jnp.where(place < 0, -1.0, jnp.where(place >= devices, 1.0, 0.0))
        parts = state_ref[feat:, :].astype(F32)
        for a in range(3):
            line = parts[a : a + 1] + parts[3 + a : 4 + a] + parts[6 + a : 7 + a]
            line = line + turn * lattice_ref[0, a]
            for q in range(tiles):
                window_ref[j * tiles + q, a : a + 1, :] = line[:, q * LANES : (q + 1) * LANES]
    padded = first_w.shape[1]
    starts[...] = row_starts(padded)
    order = row_order(padded).astype(BF16)
    for l in range(layers):
        bias = column(ffb_ref[l : l + 1, :], feat)[:, 0:1]
        high = bias.astype(BF16)
        middle = (bias - high.astype(F32)).astype(BF16)
        low = (bias - high.astype(F32) - middle.astype(F32)).astype(BF16)
        rest = jnp.zeros((feat, padded - nbasis - 3), BF16)
        weight = jnp.concatenate([ff_ref[l], high, middle, low, rest], axis=1)
        first_w[l * feat : (l + 1) * feat, :] = dot(weight, order).astype(BF16)
    second_w[...] = turned(fs_ref[0])
    second_b[...] = column(fsb_ref[0:1, :], feat)

    def target_of(index):
        return split_key(keys_ref[pl.ds(index, 1), :], source_bits, own_bits)[1]

    pooling = Pooling(total, message, target_of, info_ref, ids)
    passes = pass_count(info_ref)
    own_window = window_ref.at[center * tiles : (center + 1) * tiles]

    static = 9
    groups = keys_ref.shape[0] // PASS

    def span_of(g):
        chunks = info_ref[COUNT, 0] - g * PASS
        first, last = info_ref[FIRST, g * PASS], info_ref[LAST, g * PASS]
        for u in range(1, PASS):
            lowest, highest = info_ref[FIRST, g * PASS + u], info_ref[LAST, g * PASS + u]
            first = jnp.where(u < chunks, jnp.minimum(first, lowest), first)
            last = jnp.where(u < chunks, jnp.maximum(last, highest), last)
        return first, last

    def geometry(g, into, loop):
        rows = pl.ds(pl.multiple_of(g * PASS, PASS), PASS)
        key = keys_ref[rows, :]
        source, target = split_key(key, source_bits, own_bits)
        first, last = span_of(g)

        def pick(ref, index, places, fill):
            low = index & (LANES - 1)
            high = index >> 7
            out = list(fill)
            for b in places:
                inside = high == b
                for a in range(3):
                    line = jnp.broadcast_to(ref[b, a : a + 1, :], (8, LANES))
                    got = [
                        gather_lanes(line, low[:, q * LANES : (q + 1) * LANES])
                        for q in range(tiles_wide)
                    ]
                    out[a] = jnp.where(inside, joined(got), out[a])
            return tuple(out)

        zero = (jnp.zeros(key.shape, F32),) * 3
        there = zero
        for begin in range(0, static, 3):
            there = pick(window_ref, source, [first + begin + b for b in range(3)], there)
            yield
        if loop:
            there = lax.fori_loop(
                first + static, last + 1, lambda b, got: pick(window_ref, source, [b], got), there
            )
        here = pick(own_window, target, range(tiles), zero)
        yield
        image_one = (((key >> 2) & 3) - 1).astype(F32)
        image_two = ((key & 3) - 1).astype(F32)
        square = 0.0
        for a in range(3):
            gap = there[a] + image_one * lattice_ref[1, a] + image_two * lattice_ref[2, a] - here[a]
            square = square + gap * gap
        distance = jnp.sqrt(square)
        half_wave = 0.5 * (jnp.cos(distance * (math.pi / RADIUS)) + 1.0)
        alive = (distance < RADIUS) & (key < LIVE_BOUND)
        weight = jnp.where(alive, half_wave, 0.0)
        dist_ref[into] = distance
        weight_ref[into] = weight


    interleave([geometry(0, 0, True)])

    def one_pass(p, slot):

        coming = jnp.minimum(p + 1, groups - 1)

        def chunk(item, mode):
            u, index, first, last, half = item
            source_row = split_key(keys_ref[pl.ds(index, 1), :], source_bits, own_bits)[0]
            basis = radial(dist_ref[p, u : u + 1, :], starts[...], nbasis, padded, True)
            yield
            scaled = (dot(first_w[...], basis) * LOG2E).astype(BF16)
            pre_buf[slot, u] = scaled[feat:]
            yield
            hidden, slope = activation(scaled[:feat])
            hidden_buf[slot, u] = hidden
            slope_buf[slot, u] = slope
            yield
            filters = dot(second_w[...], hidden) + widened(second_b[...], tiles_wide)
            filters = filters.astype(BF16) * weight_ref[p, u : u + 1, :].astype(BF16)
            filter_buf[slot, u] = filters
            yield
            rows = gather_sources(table, source_row, first, last, mode)
            rows_buf[slot, u] = rows
            yield
            message[:, pooling.span(u)] = rows * filters
            yield

        each_pass(p, info_ref, chunk, pooling, lambda: geometry(coming, p + 1, False))
        first, last = span_of(coming)
        beside = is_whole(p, info_ref) & (last - first < static)

        @pl.when((p + 1 < passes) & jnp.logical_not(beside))
        def _():
            interleave([geometry(coming, p + 1, True)])

    stores = [
        Flow(far, near, sems.at[i], store=True)
        for i, (far, near) in enumerate(
            (
                (hidden_far, hidden_buf),
                (slope_far, slope_buf),
                (filter_far, filter_buf),
                (rows_far, rows_buf),
                (pre_far, pre_buf),
            )
        )
    ]
    flow_loop(passes, [], stores, one_pass)
    pooling.finish(passes - 1)

    pooled = pooling.rows()
    pre, hidden, branch = atom_forward(
        pooled, af_ref[0], afb_ref[0:1, :], as_ref[0], asb_ref[0:1, :]
    )
    state = own_ref[...] + branch
    next_ref[...] = state
    low_ref[...] = state.astype(BF16)
    kept_ref[0:feat, :] = pooled.astype(F32)
    kept_ref[feat : 2 * feat, :] = pre
    kept_ref[2 * feat : 3 * feat, :] = hidden.astype(F32)
    wait_last(passes, stores)


def top_kernel(
    source_bits,
    own_bits,
    state_refs,
    sums_refs,
    info_ref,
    keys_ref,
    weight_ref,
    own_ref,
    cot_ref,
    proj_ref,
    fs_ref,
    fsb_ref,
    af_ref,
    afb_ref,
    as_ref,
    asb_ref,
    arg_far,
    out_ref,
    pack_ref,
    low_far,
    ids,
    table,
    total,
    message,
    rows_keep,
    filter_keep,
    hidden_keep,
    slope_keep,
    target_table,
    source_total,
    second_total,
    second_w,
    second_b,
    arg_buf,
    low_buf,
    sems,
):
    feat, own = own_ref.shape
    tiles = own // LANES
    passes = pass_count(info_ref)

    ids[...] = row_numbers()
    arg_flow = Flow(arg_far, arg_buf, sems.at[0])
    start_first([arg_flow])
    build_sources(table, proj_ref[1], state_refs)
    second_w[...] = turned(fs_ref[1])
    second_b[...] = column(fsb_ref[1:2, :], feat)
    source_total[...] = jnp.zeros(source_total.shape, F32)
    second_total[...] = jnp.zeros(second_total.shape, F32)
    pack_ref[...] = jnp.zeros(pack_ref.shape, F32)

    tiles_wide = keys_ref.shape[1] // LANES

    def target_of(index):
        return split_key(keys_ref[pl.ds(index, 1), :], source_bits, own_bits)[1]

    pooling = Pooling(total, message, target_of, info_ref, ids)

    def forward(p, slot):
        def chunk(item, mode):
            u, index, first, last, half = item
            source_row = split_key(keys_ref[pl.ds(index, 1), :], source_bits, own_bits)[0]
            hidden, slope = activation(arg_buf[slot, u])
            hidden_keep[index] = hidden
            slope_keep[index] = slope
            yield
            filters = dot(second_w[...], hidden) + widened(second_b[...], tiles_wide)
            filters = filters.astype(BF16) * weight_ref[p, u : u + 1, :].astype(BF16)
            filter_keep[index] = filters
            yield
            rows = gather_sources(table, source_row, first, last, mode)
            rows_keep[index] = rows
            yield
            message[:, pooling.span(u)] = rows * filters
            yield

        each_pass(p, info_ref, chunk, pooling)

    flow_loop(passes, [arg_flow], [], forward)
    pooling.finish(passes - 1)

    pooled = pooling.rows()
    pre, hidden, branch = atom_forward(
        pooled, af_ref[1], afb_ref[1:2, :], as_ref[1], asb_ref[1:2, :]
    )
    out_ref[...] = own_ref[...] + branch
    grad = atom_backward(cot_ref[...], pooled, pre, hidden, af_ref[1], as_ref[1], pack_ref)
    store_targets(target_table, grad)

    def backward(p, slot):
        def chunk(item, mode):
            u, index, first, last, half = item
            key = keys_ref[pl.ds(index, 1), :]
            source_row, target_row = split_key(key, source_bits, own_bits)
            grads = gather_targets(target_table, target_row, half)
            yield
            filter_grad = grads * rows_keep[index] * weight_ref[p, u : u + 1, :].astype(BF16)
            spread = grads * filter_keep[index]
            yield
            low_buf[slot, u] = second_grads(
                hidden_keep[index], slope_keep[index], filter_grad, fs_ref[1], second_total
            )
            yield
            add_to_sources(source_total, spread, source_row, first, last, mode, ids[...])
            yield

        each_pass(p, info_ref, chunk)

    stores = [Flow(low_far, low_buf, sems.at[1], store=True)]
    flow_loop(passes, [], stores, backward)
    pack_ref[0:feat, :] = source_product(state_refs, source_total, sums_refs)
    pack_ref[3 * (feat + 8) :, :] = second_total[...]
    wait_last(passes, stores)


def low_kernel(
    source_bits,
    own_bits,
    nbasis,
    state_refs,
    source_refs,
    ends_refs,
    sums_pair_refs,
    info_ref,
    keys_ref,
    dist_ref,
    weight_ref,
    cot_ref,
    proj_ref,
    fs_ref,
    af_ref,
    as_ref,
    kept_ref,
    top_pack_ref,
    hidden_far,
    slope_far,
    filter_far,
    rows_far,
    low_far,
    out_ref,
    grad_ref,
    ids,
    starts,
    pack,
    target_table,
    flat,
    source_total,
    first_total,
    second_total,
    hidden_buf,
    slope_buf,
    filter_buf,
    rows_buf,
    low_buf,
    sems,
):
    feat = cot_ref.shape[0]
    loads = [
        Flow(far, near, sems.at[i])
        for i, (far, near) in enumerate(
            (
                (hidden_far, hidden_buf),
                (slope_far, slope_buf),
                (filter_far, filter_buf),
                (rows_far, rows_buf),
                (low_far, low_buf),
            )
        )
    ]
    start_first(loads)
    ids[...] = row_numbers()
    padded = first_total.shape[0]
    starts[...] = row_starts(padded)
    pack[...] = jnp.zeros(pack.shape, F32)
    source_total[...] = jnp.zeros(source_total.shape, F32)
    first_total[...] = jnp.zeros(first_total.shape, F32)
    second_total[...] = jnp.zeros(second_total.shape, F32)
    source = summed(source_refs).astype(BF16)
    grad = cot_ref[...] + dot(proj_ref[1], source)
    grad_ref[...] = grad
    pooled = kept_ref[0:feat, :].astype(BF16)
    hidden = kept_ref[2 * feat : 3 * feat, :].astype(BF16)
    pooled_grad = atom_backward(
        grad, pooled, kept_ref[feat : 2 * feat, :], hidden, af_ref[0], as_ref[0], pack
    )
    store_targets(target_table, pooled_grad)

    def one_pass(p, slot):
        def chunk(item, mode):
            u, index, first, last, half = item
            key = keys_ref[pl.ds(index, 1), :]
            source_row, target_row = split_key(key, source_bits, own_bits)
            grads = gather_targets(target_table, target_row, half)
            yield
            filter_grad = grads * rows_buf[slot, u] * weight_ref[p, u : u + 1, :].astype(BF16)
            spread = grads * filter_buf[slot, u]
            yield
            low = second_grads(
                hidden_buf[slot, u], slope_buf[slot, u], filter_grad, fs_ref[0], second_total
            )
            low = jnp.concatenate([low, low_buf[slot, u]], axis=0)
            yield
            basis = radial(dist_ref[p, u : u + 1, :], starts[...], nbasis, padded, True)
            yield
            first_total[...] += dot_nt(basis, low)
            yield
            add_to_sources(source_total, spread, source_row, first, last, mode, ids[...])
            yield

        each_pass(p, info_ref, chunk)

    flow_loop(pass_count(info_ref), loads, [], one_pass)
    sums_refs = sums_views(ends_refs, sums_pair_refs, feat)
    pack[0:feat, :] = source_product(state_refs, source_total, sums_refs)
    pack[3 * (feat + 8) :, :] = second_total[...]
    write_packs(out_ref, flat, first_total, (pack[...], top_pack_ref[...]))


def summed(refs):
    return sum(ref[...].astype(F32) for ref in refs)


def add_kernel(pair_refs, rank_ref, lower_ref, own_ref, upper_ref, parts_ref, copies_ref, *out_refs):
    devices = parts_ref.shape[0]
    total = sum(parts_ref[d].astype(F32) for d in range(devices)).astype(BF16)
    for d in range(devices):
        copies_ref[d] = total
    gathered_sums(rank_ref, lower_ref, own_ref, upper_ref, pair_refs, *out_refs)


def last_kernel(
    padded,
    source_refs,
    copies_ref,
    grad_ref,
    proj_ref,
    feature_ref,
    proj_grad_ref,
    ff_ref,
    ffb_ref,
    fs_ref,
    fsb_ref,
    af_ref,
    afb_ref,
    as_ref,
    asb_ref,
    flat,
):
    devices, share, _ = copies_ref.shape
    layers, feat, nbasis = ff_ref.shape
    part = feat + 8

    for d in range(devices):
        flat[d * share : (d + 1) * share, :] = copies_ref[d].astype(F32)
    for l in range(layers):
        base = l * padded
        ff_ref[l] = flat[base : base + padded, :].T[0:feat, 0:nbasis]
        ffb_ref[l : l + 1, :] = flat[base + nbasis : base + nbasis + 1, 0:feat]
        proj_grad_ref[l] = flat[base : base + feat, feat : 2 * feat]
        for place, weight_ref, bias_ref in (
            (part, af_ref, afb_ref),
            (2 * part, as_ref, asb_ref),
            (3 * part, fs_ref, fsb_ref),
        ):
            at = base + place
            weight_ref[l] = flat[at : at + feat, feat : 2 * feat]
            bias_ref[l : l + 1, :] = flat[at + feat : at + feat + 1, feat : 2 * feat]
    source = summed(source_refs).astype(BF16)
    feature_ref[...] = grad_ref[...] + dot(proj_ref[0], source)


def moved(value, axis, steps):
    count = lax.axis_size(axis)
    return lax.ppermute(value, axis, [(i, (i + steps) % count) for i in range(count)])


def around(steps, blocks):
    axes = ("edges", "grp")
    count = lax.axis_size("edges") * lax.axis_size("grp")
    out = []
    for step, block in zip(steps, blocks):
        pairs = [(i, (i + step) % count) for i in range(count)]
        out.append(block if step == 0 else lax.ppermute(block, axes, pairs))
    return out


def grouped(kernel, *counts):
    def run(*refs):
        lists, at = [], 0
        for count in counts:
            lists.append(refs[at : at + count])
            at += count
        kernel(*lists, *refs[at:])

    return run


def across(value):
    return lax.all_to_all(value, ("edges", "grp"), split_axis=0, concat_axis=0, tiled=True)


def on_device(
    features,
    positions,
    lattice,
    neighbour_source,
    neighbour_image,
    valid_count,
    input_proj,
    filter_first,
    filter_first_bias,
    filter_second,
    filter_second_bias,
    atom_first,
    atom_first_bias,
    atom_second,
    atom_second_bias,
    cotangent,
):
    feat, own = features.shape
    slot_rows, slab = neighbour_source.shape
    layers, nbasis, _ = filter_first.shape
    group = lax.axis_size("grp")
    slabs = lax.axis_size("edges")
    devices = group * slabs
    rank = lax.axis_index("grp")
    slab_id = lax.axis_index("edges")
    slots = slot_rows * group
    own_bits = own.bit_length() - 1
    reach = slab
    window = 2 * reach + own
    blocks = window // LANES
    source_bits = (window - 1).bit_length()
    tiles = own // LANES
    chunk = own * slots // LANES
    chunks = LANES + 8
    padded = -(-nbasis // 16) * 16
    both = layers * feat
    part = feat + 8
    pack_height = 3 * part + feat + 16
    share = -(-layers * padded // (8 * devices)) * 8
    others = group - 1
    near = [*range(-group, 0), *range(group, 0, -1), 0]
    inward = [*range(-1, -group - 1, -1), *range(1, group + 1), 0]
    outward = [-step for step in inward]
    count = len(near)

    def in_order(refs, listed=near):
        return [refs[listed.index(step)] for step in sorted(near)]


    vmem = pl.BlockSpec(memory_space=pltpu.VMEM)
    smem = pl.BlockSpec(memory_space=pltpu.SMEM)
    far = pl.BlockSpec(memory_space=pl.ANY)

    def call(kernel, outs, out_specs, in_specs, args, scratch, flops, vmem_mib):
        return pl.pallas_call(
            kernel,
            out_shape=outs,
            in_specs=in_specs,
            out_specs=out_specs,
            scratch_shapes=scratch,
            compiler_params=pltpu.CompilerParams(vmem_limit_bytes=vmem_mib * MIB),
            cost_estimate=pl.CostEstimate(
                flops=flops, bytes_accessed=flops // 1000, transcendentals=0
            ),
        )(*args)

    def cube(dtype=BF16):
        return jax.ShapeDtypeStruct((chunks, feat, chunk), dtype)

    def buffer(dtype=BF16):
        return pltpu.VMEM((2, PASS, feat, chunk), dtype)

    flat = jax.ShapeDtypeStruct((chunks // PASS + 1, PASS, chunk), F32)
    own_f32 = jax.ShapeDtypeStruct((feat, own), F32)
    own_bf16 = jax.ShapeDtypeStruct((feat, own), BF16)
    pack_shape = jax.ShapeDtypeStruct((pack_height, feat), F32)
    whole_pack = jax.ShapeDtypeStruct((devices, share, both), BF16)
    flat_rows = pltpu.VMEM((devices * share, both), F32)
    work = 1 << 33

    ids = pltpu.VMEM((LANES, LANES), BF16)
    table = pltpu.VMEM((blocks + 3, feat, LANES), BF16)
    total = pltpu.VMEM((2, LANES, tiles // 2 * feat), F32)
    message = pltpu.VMEM((feat, PASS * chunk), BF16)
    starts = pltpu.VMEM((8, LANES), F32)
    target_table = pltpu.VMEM((tiles, feat, LANES), BF16)
    source_total = pltpu.VMEM((blocks + 3, feat, LANES), F32)
    first_total = pltpu.VMEM((padded, both), F32)
    second_total = pltpu.VMEM((feat + 16, feat), F32)
    small = pltpu.VMEM((feat, feat), BF16)
    bias = pltpu.VMEM((feat, LANES), F32)

    def sems(count):
        return pltpu.SemaphoreType.DMA((count, 2))

    rank_info = rank.reshape(1).astype(jnp.int32)
    sent = (rank_info, neighbour_source, neighbour_image, features)
    words, block0 = call(
        send_kernel,
        (
            jax.ShapeDtypeStruct((group, 3, slot_rows, own), jnp.int16),
            jax.ShapeDtypeStruct((feat + 16, own), BF16),
        ),
        (vmem, vmem),
        [smem] + [vmem] * 4,
        (*sent, positions),
        [],
        work,
        56,
    )
    words = lax.all_to_all(words, "grp", split_axis=0, concat_axis=0, tiled=True)
    state0 = around(outward, [block0] * count)
    valid = valid_count.reshape(1, slab)
    device_id = (slab_id * group + rank).reshape(1).astype(jnp.int32)

    keys, info = call(
        functools.partial(sort_kernel, reach, source_bits, own_bits),
        (
            jax.ShapeDtypeStruct((chunks, chunk), jnp.int32),
            jax.ShapeDtypeStruct((8, 2 * LANES), jnp.int32),
        ),
        (pl.BlockSpec(memory_space=pltpu.HBM), vmem),
        [smem] + [vmem] * 2,
        (rank_info, words, valid),
        [pltpu.VMEM((chunks, chunk), jnp.int32), pltpu.SemaphoreType.DMA],
        work,
        16,
    )

    turned_first = filter_first.transpose(0, 2, 1)
    filter_weights = (turned_first, filter_first_bias, filter_second, filter_second_bias)
    atom_weights = (atom_first, atom_first_bias, atom_second, atom_second_bias)
    first_args = (info, lattice, device_id, keys, features, input_proj)
    first_args = first_args + filter_weights + atom_weights
    def first(*refs):
        state_refs = in_order(refs[:count], inward)
        first_kernel(source_bits, own_bits, nbasis, devices, state_refs, *refs[count:])

    outs = (flat, flat, cube(), cube(), cube(), cube(), cube())
    outs = outs + (own_f32, own_bf16, jax.ShapeDtypeStruct((3 * feat, own), F32))
    (
        dist,
        edge_weight,
        hidden0,
        slope0,
        filter0,
        rows0,
        arg1,
        state1,
        low1,
        kept0,
    ) = call(
        first,
        outs,
        (vmem, vmem) + (far,) * 5 + (vmem,) * 3,
        [vmem] * len(state0) + [smem] * 3 + [vmem] * (len(first_args) - 3),
        (*state0, *first_args),
        [ids, pltpu.VMEM((blocks + 9, 8, LANES), F32), table]
        + [total, message, starts]
        + [pltpu.VMEM((both, padded), BF16), small, bias]
        + [buffer()] * 4
        + [buffer(), sems(5)],
        4 * work,
        53,
    )

    state1_blocks = around(outward, [low1] * count)

    top_args = (info, keys, edge_weight, state1, cotangent, input_proj, filter_second)
    top_args = top_args + (filter_second_bias,) + atom_weights
    kept = pltpu.VMEM((chunks, feat, chunk), BF16)

    sums_shapes = (own_bf16,) * 3 + (jax.ShapeDtypeStruct((2 * feat, own), BF16),) * others

    def split(refs, *counts):
        lists, at = [], 0
        for count in counts:
            lists.append(refs[at : at + count])
            at += count
        return (*lists, refs[at:])

    def top(*refs):
        state_refs, inputs, sums_refs, rest = split(refs, count, len(top_args) + 1, count)
        top_kernel(
            source_bits,
            own_bits,
            in_order(state_refs, inward),
            in_order(sums_refs),
            *inputs,
            *rest,
        )

    *sums1, new_features, pack1, low1_grad = call(
        top,
        (own_bf16,) * count + (own_f32, pack_shape, cube()),
        (vmem,) * (count + 2) + (far,),
        [vmem] * count + [smem] + [vmem] * (len(top_args) - 1) + [far],
        (*state1_blocks, *top_args, arg1),
        [ids, table, total, message, kept, kept, kept, kept, target_table]
        + [source_total, second_total, small, bias, buffer(), buffer(), sems(2)],
        4 * work,
        53,
    )

    source1 = around(near, sums1)

    low_args = (info, keys, dist, edge_weight, cotangent, input_proj, filter_second)
    low_args = low_args + (atom_first, atom_second, kept0, pack1)

    def low(*refs):
        state_refs, source_refs, inputs, ends_refs, sums_pair_refs, rest = split(
            refs, count, count, len(low_args) + 5, 3, others
        )
        low_kernel(
            source_bits,
            own_bits,
            nbasis,
            in_order(state_refs, inward),
            source_refs,
            ends_refs,
            sums_pair_refs,
            *inputs,
            *rest,
        )

    *sums0, grads, grad = call(
        low,
        sums_shapes + (whole_pack, own_f32),
        (vmem,) * (group + 4),
        [vmem] * (2 * count) + [smem] + [vmem] * (len(low_args) - 1) + [far] * 5,
        (*state0, *source1, *low_args, hidden0, slope0, filter0, rows0, low1_grad),
        [ids, starts, pltpu.VMEM(pack_shape.shape, F32), target_table, flat_rows, source_total]
        + [first_total, second_total]
        + [buffer()] * 5
        + [sems(5)],
        4 * work,
        53,
    )

    pairs0 = [moved(pair, "grp", s) for s, pair in enumerate(sums0[3:], 1)]
    totals = (own_f32, own_bf16, own_bf16)
    copies, mine, below, above = call(
        grouped(add_kernel, others),
        (whole_pack,) + totals,
        (vmem,) * 4,
        [vmem] * others + [smem] + [vmem] * 4,
        (*pairs0, rank_info, *sums0[:3], across(grads)),
        [],
        work,
        16,
    )
    weights = (input_proj,) + filter_weights + atom_weights
    feature_grad, *weight_grads = call(
        grouped(functools.partial(last_kernel, padded), 3),
        (own_f32,) + tuple(jax.ShapeDtypeStruct(w.shape, F32) for w in weights),
        (vmem,) * 10,
        [vmem] * 6,
        (mine, moved(below, "edges", -1), moved(above, "edges", 1), across(copies), grad)
        + (input_proj,),
        [flat_rows],
        work,
        16,
    )
    first_grad = weight_grads[1].transpose(0, 2, 1)
    return (new_features, feature_grad, weight_grads[0], first_grad, *weight_grads[2:])


def solution(mesh):
    in_specs = (
        P(None, ("edges", "grp")),
        P(None, "edges"),
        P(),
        P("grp", "edges"),
        P(None, "grp", "edges"),
        P("edges"),
        P(),
        P(),
        P(),
        P(),
        P(),
        P(),
        P(),
        P(),
        P(),
        P(None, ("edges", "grp")),
    )
    out_specs = (P(None, ("edges", "grp")), P(None, ("edges", "grp"))) + (P(),) * 9
    return jax.shard_map(
        on_device, mesh=mesh, in_specs=in_specs, out_specs=out_specs, check_vma=False
    )
```
